128 devices in a mesh: freq: 16 (over y, x_lo, core), row: 2 (over x_hi), col: 4 (over z).
Axes of the slice: x: 4 (x_hi: 2, x_lo: 2; x = x_hi * 2 + x_lo), y: 4, z: 4, core: 2. Of those that a mesh axis runs over, the one named last changes fastest.
Arguments:
- voltages: bfloat16 [512, 256, 2048], P(('row', 'col'), 'freq'), may hold values from -6 to 6
- window: float32 [16, 2048], replicated, may hold values from -1.5 to 1.5
Outputs:
- vis_real: float32 [1024, 512, 512], P('freq', 'row', 'col')
- vis_imag: float32 [1024, 512, 512], P('freq', 'row', 'col')
The draws below stay inside these ranges and needn't reach their ends.
All inputs are finite; a program needn't handle non-finite values.
Results may differ from the reference program's by a relative error of at most 0.007.
Values may be sent and summed in bfloat16 or wider, within the bound.
No kernel may reach another device: no remote copies, remote signals or barrier semaphores. Data moves between devices by JAX's collectives and lax.ppermute only.
A program may use at most 192 MiB of HBM per device.

```python
import math
import jax
import jax.numpy as jnp
from jax import lax

INPUTS = 512
NFFT = 2048
TAPS = 16
SPECTRA = 256
CHAN = 1024
IN_DEV = 64
N_ROW = 2
N_COL = 4


def block_levels(own_key, shape, cuts, smallest, largest):
    gain = 1.0
    for position, blocks in cuts:
        heights = jax.random.uniform(jax.random.fold_in(jax.random.fold_in(own_key, 6), position), (blocks,), jnp.float32, smallest / len(cuts), largest / len(cuts))
        gain = gain * jnp.repeat(jnp.exp(heights), shape[position] // blocks).reshape((-1,) + (1,) * (len(shape) - 1 - position))
    return gain


def noise(own_key, extent, spread, limit, pieces=(), held_as=jnp.bfloat16):
    loudness = block_levels(own_key, extent, pieces, -0.22, 0.18) if pieces else 1.0
    entries = jax.random.normal(own_key, extent, jnp.float32) * spread * loudness
    return jnp.minimum(jnp.maximum(entries, -limit), limit).astype(held_as)


def setup_inputs(seed: int = 0) -> dict:
    streams_of = jax.random.split(jax.random.key(seed), 3)
    return {
        "voltages": noise(streams_of[0], (INPUTS, SPECTRA, NFFT), 1.0, 6.0, ((0, 8), (1, 16))),
        "window": noise(streams_of[1], (TAPS, NFFT), TAPS ** -0.5, 1.5, (), jnp.float32),
    }


def make_table(length):
    rows = lax.broadcasted_iota(jnp.int32, (length, length), 0)
    cols = lax.broadcasted_iota(jnp.int32, (length, length), 1)
    phase = rows * (cols // 2) % length
    angle = phase.astype(jnp.float32) * (2.0 * math.pi / length)
    values = jnp.where(cols % 2 == 0, jnp.cos(angle), -jnp.sin(angle))
    return (values / math.sqrt(length)).astype(jnp.bfloat16)

def reference(voltages, window):
    table = make_table(NFFT)
    groups = voltages.reshape(INPUTS // 8, 8, SPECTRA, NFFT)

    def channelize(block):
        padded = jnp.concatenate([block, jnp.zeros((8, TAPS - 1, NFFT), jnp.bfloat16)], axis=1)
        total = jnp.zeros((8, SPECTRA, NFFT), jnp.float32)
        for k in range(TAPS):
            total = total + window[k][None, None, :] * padded[:, k:k + SPECTRA, :].astype(jnp.float32)
        filtered = total.astype(jnp.bfloat16).reshape(8 * SPECTRA, NFFT)
        result = jnp.dot(filtered, table, preferred_element_type=jnp.float32)
        return result.astype(jnp.bfloat16).reshape(8, SPECTRA, NFFT)
    spectra = lax.map(channelize, groups).reshape(INPUTS, SPECTRA, NFFT)
    arranged = spectra.reshape(INPUTS, SPECTRA, CHAN, 2).transpose(2, 0, 1, 3)
    index = jnp.arange(INPUTS, dtype=jnp.int32)
    perm = index // IN_DEV % N_ROW * (N_COL * IN_DEV) + index // (N_ROW * IN_DEV) * IN_DEV + index % IN_DEV
    second = arranged[:, perm]
    rotated = jnp.stack([-second[..., 1], second[..., 0]], axis=-1)
    first = arranged.reshape(CHAN // 8, 8, INPUTS, 2 * SPECTRA)
    second = second.reshape(CHAN // 8, 8, INPUTS, 2 * SPECTRA)
    rotated = rotated.reshape(CHAN // 8, 8, INPUTS, 2 * SPECTRA)

    def correlate(triple):
        left, right, turned = triple
        left = left.astype(jnp.float32)
        real_part = jnp.einsum('cak,cbk->cab', left, right.astype(jnp.float32))
        imag_part = jnp.einsum('cak,cbk->cab', left, turned.astype(jnp.float32))
        return (real_part / SPECTRA, imag_part / SPECTRA)
    vis_real, vis_imag = lax.map(correlate, (first, second, rotated))
    return (vis_real.reshape(CHAN, INPUTS, INPUTS), vis_imag.reshape(CHAN, INPUTS, INPUTS))
```

```python
import functools
import math

import jax
import jax.numpy as jnp
import ml_dtypes
import numpy as np
from jax import lax
from jax.experimental import pallas as pl
from jax.experimental.pallas import tpu as pltpu
from jax.sharding import PartitionSpec as P

LANES = 128
CHUNKS = 4
COLS = 256


def dft_table(length, groups):
    half = length // 2
    width = half // groups
    base = np.arange(length) * (2.0 * math.pi / length)
    cosine = np.cos(base) / math.sqrt(length)
    sine = -np.sin(base) / math.sqrt(length)
    phase = np.arange(length)[:, None] * np.arange(half)[None, :] % length
    parts = np.stack([cosine[phase], sine[phase]], axis=1)
    parts = parts.reshape(length, 2, groups, width).transpose(2, 0, 1, 3)
    blocks = parts.reshape(groups // 2, 2, length, 2 * width).transpose(0, 2, 1, 3)
    return blocks.reshape(groups // 2, length, 4 * width).astype(ml_dtypes.bfloat16)


def channelize_kernel(v_ref, h_ref, w_ref, t_ref, u_ref, ext, acc, filt):
    n_in, frames, length = v_ref.shape
    taps = w_ref.shape[0]
    depth = 2 * frames

    @pl.when(pl.program_id(0) == 0)
    def _():
        def one_tile(t, carry):
            lanes = pl.ds(pl.multiple_of(t * LANES, LANES), LANES)
            for i in range(n_in):
                ext[pl.ds(i * depth, frames), :] = v_ref[i, :, lanes].astype(jnp.float32)
                ext[pl.ds(i * depth + frames, frames), :] = h_ref[i, :, lanes].astype(jnp.float32)
            weights = [w_ref[pl.ds(k, 1), lanes] for k in range(taps)]
            weights = [jnp.broadcast_to(w, (8, LANES)) for w in weights]
            for g in range(n_in // 8):
                x = [ext[pl.ds(g * 8 * depth + s, 8, stride=depth), :] for s in range(frames + taps - 1)]
                for s in range(frames):
                    total = weights[0] * x[s]
                    for k in range(1, taps):
                        total = total + weights[k] * x[s + k]
                    acc[pl.ds(g * 8 * frames + s, 8, stride=frames), :] = total
            filt[:, lanes] = acc[...].astype(jnp.bfloat16)
            return carry

        lax.fori_loop(0, length // LANES, one_tile, 0)

    out = jnp.dot(filt[...], t_ref[0], preferred_element_type=jnp.float32)
    out = out.astype(jnp.bfloat16)
    for j in range(u_ref.shape[0]):
        u_ref[j] = out[:, j * LANES : (j + 1) * LANES].reshape(n_in, frames, LANES)


def channelize(chunk, n_in, voltages, halo, window, table):
    frames, length = voltages.shape[1:]
    blocks = table.shape[0]
    groups = 2 * blocks
    rows = n_in * frames
    return pl.pallas_call(
        channelize_kernel,
        grid=(blocks,),
        in_specs=[
            pl.BlockSpec((n_in, frames, length), lambda b: (chunk, 0, 0)),
            pl.BlockSpec((n_in, frames, length), lambda b: (0, 0, 0)),
            pl.BlockSpec(window.shape, lambda b: (0, 0)),
            pl.BlockSpec((1, length, COLS), lambda b: (b, 0, 0)),
        ],
        out_specs=pl.BlockSpec((2, n_in, frames, LANES), lambda b: (b, 0, 0, 0)),
        out_shape=jax.ShapeDtypeStruct((groups, n_in, frames, LANES), jnp.bfloat16),
        scratch_shapes=[
            pltpu.VMEM((2 * rows, LANES), jnp.float32),
            pltpu.VMEM((rows, LANES), jnp.float32),
            pltpu.VMEM((rows, length), jnp.bfloat16),
        ],
        compiler_params=pltpu.CompilerParams(vmem_limit_bytes=32 * 2**20),
        cost_estimate=pl.CostEstimate(
            flops=2 * rows * length * length, bytes_accessed=12 * 2**20, transcendentals=0
        ),
        name="channelize",
    )(voltages, halo, window, table)


def turn_kernel(x_ref, g_ref, scr):
    devices, n_in, frames, lanes = x_ref.shape
    chans = lanes // 2
    depth = devices * frames
    for i in range(n_in):
        block = x_ref[:, i, :, :].reshape(depth, lanes).astype(jnp.float32)
        for h in range(depth // LANES):
            piece = block[h * LANES : (h + 1) * LANES, :].T
            scr[h, pl.ds(i, chans, stride=2 * n_in), :] = piece[:chans]
            scr[h, pl.ds(n_in + i, chans, stride=2 * n_in), :] = piece[chans:]
    for h in range(depth // LANES):
        g_ref[:, :, h * LANES : (h + 1) * LANES] = (
            scr[h].reshape(chans, 2 * n_in, LANES).astype(jnp.bfloat16)
        )


def turn(received):
    devices, n_in, frames, lanes = received.shape
    chans, depth = lanes // 2, devices * frames
    return pl.pallas_call(
        turn_kernel,
        out_shape=jax.ShapeDtypeStruct((chans, 2 * n_in, depth), jnp.bfloat16),
        scratch_shapes=[pltpu.VMEM((depth // LANES, chans * 2 * n_in, LANES), jnp.float32)],
        compiler_params=pltpu.CompilerParams(vmem_limit_bytes=32 * 2**20),
        cost_estimate=pl.CostEstimate(flops=10**9, bytes_accessed=4 * 2**20, transcendentals=0),
        name="turn",
    )(received)


def correlate_kernel(chunks, scale, place, *refs):
    blocks = refs[: 4 * chunks]
    swapped = refs[4 * chunks : 5 * chunks]
    re_ref, im_ref, partner = refs[5 * chunks :]
    chans, twice, depth = blocks[0].shape
    n_in = twice // 2
    inputs = n_in * chunks
    half = partner.shape[0] // 2
    for ch in range(chans):
        for row in range(2):

            @pl.when(place[0] == row)
            def _(own_at=row * inputs, far_at=(1 - row) * inputs):
                for q in range(chunks):
                    near, far = blocks[q][ch], swapped[q][ch]
                    at = q * n_in
                    partner[own_at + at : own_at + at + n_in, :] = near[:n_in]
                    partner[half + own_at + at : half + own_at + at + n_in, :] = near[n_in:]
                    partner[far_at + at : far_at + at + n_in, :] = far[:n_in]
                    partner[half + far_at + at : half + far_at + at + n_in, :] = far[n_in:]

        first = jnp.concatenate([ref[ch] for ref in blocks], axis=0)
        products = lax.dot_general(
            first, partner[...], (((1,), (1,)), ((), ())), preferred_element_type=jnp.float32
        )
        for d in range(4):
            at = pl.multiple_of(place[1 + d] * inputs, inputs)
            for q in range(chunks):
                start = (d * chunks + q) * twice
                re = products[start : start + n_in]
                im = products[start + n_in : start + twice]
                rows = pl.ds(at + q * n_in, n_in)
                re_ref[ch, rows, :] = (re[:, :half] + im[:, half:]) * scale
                im_ref[ch, rows, :] = (im[:, :half] - re[:, half:]) * scale


def correlate(place, blocks, swapped, step=4):
    chunks = len(swapped)
    chans, twice, depth = swapped[0].shape
    inputs = twice // 2 * chunks
    spec = pl.BlockSpec((step, twice, depth), lambda b, place: (b, 0, 0))
    out = pl.BlockSpec((step, 4 * inputs, 2 * inputs), lambda b, place: (b, 0, 0))
    shape = jax.ShapeDtypeStruct((chans, 4 * inputs, 2 * inputs), jnp.float32)
    return pl.pallas_call(
        functools.partial(correlate_kernel, chunks, 1.0 / depth),
        grid_spec=pltpu.PrefetchScalarGridSpec(
            num_scalar_prefetch=1,
            grid=(chans // step,),
            in_specs=[spec] * (5 * chunks),
            out_specs=[out, out],
            scratch_shapes=[pltpu.VMEM((4 * inputs, depth), jnp.bfloat16)],
        ),
        out_shape=[shape, shape],
        compiler_params=pltpu.CompilerParams(vmem_limit_bytes=40 * 2**20),
        cost_estimate=pl.CostEstimate(
            flops=2 * chans * 8 * inputs * 4 * inputs * depth,
            bytes_accessed=36 * 2**20,
            transcendentals=0,
        ),
        name="correlate",
    )(place, *blocks, *swapped)


def ring(size, distance):
    return [(i, (i + distance) % size) for i in range(size)]


def shards(voltages, window, table):
    in_dev, frames, length = voltages.shape
    n_freq, n_col = lax.axis_size("freq"), lax.axis_size("col")
    n_in = in_dev // CHUNKS
    back = [(i + 1, i) for i in range(n_freq - 1)]
    row, col = lax.axis_index("row"), lax.axis_index("col")
    up, down = ring(n_col, 1), ring(n_col, -1)
    own, below, above, across, swapped = [], [], [], [], []
    for q in range(CHUNKS):
        halo = lax.ppermute(voltages[q * n_in : (q + 1) * n_in], "freq", back)
        sent = channelize(q, n_in, voltages, halo, window, table)
        received = lax.all_to_all(sent, "freq", split_axis=0, concat_axis=0, tiled=True)
        block = turn(received)
        own.append(block)
        below.append(lax.ppermute(block, "col", up))
        above.append(lax.ppermute(block, "col", down))
        if q % 2 == 0:
            across.append(lax.ppermute(below[-1], "col", up))
        else:
            across.append(lax.ppermute(above[-1], "col", down))
        swapped.append(lax.ppermute(block, "row", ring(2, 1)))
    place = jnp.stack([row, col, (col + 3) % 4, (col + 1) % 4, (col + 2) % 4]).astype(jnp.int32)
    return tuple(correlate(place, own + below + above + across, swapped))


def solution(mesh):
    n_freq = mesh.shape["freq"]

    def run(voltages, window):
        table = jnp.asarray(dft_table(voltages.shape[2], n_freq))
        return jax.shard_map(
            shards,
            mesh=mesh,
            in_specs=(P(("row", "col"), "freq", None), P(), P()),
            out_specs=(P("freq", "row", "col"), P("freq", "row", "col")),
            check_vma=False,
        )(voltages, window, table)

    return run
```

```python
import functools
import math

import jax
import jax.numpy as jnp
import ml_dtypes
import numpy as np
from jax import lax
from jax.experimental import pallas as pl
from jax.experimental.pallas import tpu as pltpu
from jax.sharding import PartitionSpec as P

LANES = 128
CHUNKS = 4
COLS = 512
PARTS = 2
SHORT = pl.CostEstimate(flops=10**8, bytes_accessed=2**17, transcendentals=0)
VMEM = 56 * 2**20


def dft_table(length, groups):
    half = length // 2
    base = np.arange(length) * (2.0 * math.pi / length)
    cosine = np.cos(base) / math.sqrt(length)
    sine = -np.sin(base) / math.sqrt(length)
    phase = np.arange(length)[:, None] * np.arange(half)[None, :] % length
    parts = np.stack([cosine[phase], sine[phase]], axis=1)
    parts = parts.reshape(length, 2, groups, half // groups).transpose(0, 2, 1, 3)
    blocks = parts.reshape(length, length // COLS, COLS).transpose(1, 0, 2)
    return blocks.astype(ml_dtypes.bfloat16)


def channelize_kernel(v_ref, h_ref, w_ref, t_ref, *refs):
    u_ref, ext, acc, filt = refs[-4:]
    n_in, frames, length = v_ref.shape
    taps = w_ref.shape[0]
    depth = 2 * frames

    @pl.when(pl.program_id(0) == 0)
    def _():
        def one_tile(t, carry):
            lanes = pl.ds(pl.multiple_of(t * LANES, LANES), LANES)
            for i in range(n_in):
                ext[pl.ds(i * depth, frames), :] = v_ref[i, :, lanes].astype(jnp.float32)
                ext[pl.ds(i * depth + frames, frames), :] = h_ref[i, :, lanes].astype(jnp.float32)
            weights = [jnp.broadcast_to(w_ref[pl.ds(k, 1), lanes], (8, LANES)) for k in range(taps)]
            for i in range(n_in):
                for s in range(0, frames, 8):
                    at = i * depth + s
                    total = weights[0] * ext[pl.ds(at, 8), :]
                    for k in range(1, taps):
                        total = total + weights[k] * ext[pl.ds(at + k, 8), :]
                    acc[pl.ds(i * frames + s, 8), :] = total
            filt[:, lanes] = acc[...].astype(jnp.bfloat16)
            return carry

        lax.fori_loop(0, length // LANES, one_tile, 0)

    out = jnp.dot(filt[...], t_ref[0], preferred_element_type=jnp.float32)
    out = out.astype(jnp.bfloat16)
    for j in range(u_ref.shape[0]):
        u_ref[j] = out[:, j * LANES : (j + 1) * LANES].reshape(n_in, frames, LANES)


def channelize(chunk, n_in, voltages, halo, window, table, earlier):
    frames, length = voltages.shape[1:]
    blocks = table.shape[0]
    rows = n_in * frames
    return pl.pallas_call(
        channelize_kernel,
        grid=(blocks,),
        in_specs=[
            pl.BlockSpec((n_in, frames, length), lambda b: (chunk, 0, 0)),
            pl.BlockSpec((n_in, frames, length), lambda b: (0, 0, 0)),
            pl.BlockSpec(window.shape, lambda b: (0, 0)),
            pl.BlockSpec((1, length, COLS), lambda b: (b, 0, 0)),
            *[pl.BlockSpec(memory_space=pl.ANY)] * len(earlier),
        ],
        out_specs=pl.BlockSpec((COLS // LANES, n_in, frames, LANES), lambda b: (b, 0, 0, 0)),
        out_shape=jax.ShapeDtypeStruct((length // LANES, n_in, frames, LANES), jnp.bfloat16),
        scratch_shapes=[
            pltpu.VMEM((2 * rows, LANES), jnp.float32),
            pltpu.VMEM((rows, LANES), jnp.float32),
            pltpu.VMEM((rows, length), jnp.bfloat16),
        ],
        compiler_params=pltpu.CompilerParams(vmem_limit_bytes=VMEM),
        cost_estimate=SHORT,
        name="channelize",
    )(voltages, halo, window, table, *earlier)


def turn_kernel(parts, x_ref, *refs):
    g_refs, scr = refs[-1 - parts : -1], refs[-1]
    devices, n_in, frames, lanes = x_ref.shape
    chans = lanes // 2
    depth = devices * frames
    part = chans // len(g_refs)
    for i in range(n_in):
        block = x_ref[:, i, :, :].reshape(depth, lanes).astype(jnp.float32)
        for h in range(depth // LANES):
            piece = block[h * LANES : (h + 1) * LANES, :].T
            scr[h, pl.ds(i, chans, stride=2 * n_in), :] = piece[:chans]
            scr[h, pl.ds(n_in + i, chans, stride=2 * n_in), :] = piece[chans:]
    for h in range(depth // LANES):
        for j, g_ref in enumerate(g_refs):
            rows = scr[h, j * part * 2 * n_in : (j + 1) * part * 2 * n_in, :]
            g_ref[:, :, h * LANES : (h + 1) * LANES] = rows.reshape(part, 2 * n_in, LANES).astype(jnp.bfloat16)


def turn(received, earlier, parts):
    devices, n_in, frames, lanes = received.shape
    chans, depth = lanes // 2, devices * frames
    shape = jax.ShapeDtypeStruct((chans // parts, 2 * n_in, depth), jnp.bfloat16)
    vmem = pl.BlockSpec(memory_space=pltpu.VMEM)
    return pl.pallas_call(
        functools.partial(turn_kernel, parts),
        in_specs=[vmem] + [pl.BlockSpec(memory_space=pl.ANY)] * len(earlier),
        out_specs=[vmem] * parts,
        out_shape=[shape] * parts,
        scratch_shapes=[pltpu.VMEM((depth // LANES, chans * 2 * n_in, LANES), jnp.float32)],
        compiler_params=pltpu.CompilerParams(vmem_limit_bytes=VMEM),
        cost_estimate=SHORT,
        name="turn",
    )(received, *earlier)


def correlate_kernel(chunks, scale, place, *refs):
    blocks = refs[: 4 * chunks]
    swapped = refs[4 * chunks : 5 * chunks]
    re_ref, im_ref = refs[-2:]
    chans, twice, depth = blocks[0].shape
    n_in = twice // 2
    inputs = n_in * chunks
    half = 2 * inputs
    low = place[0] == 0
    for ch in range(chans):
        near = [ref[ch] for ref in blocks[:chunks]]
        far = [ref[ch] for ref in swapped]
        partner = []
        for part in (slice(0, n_in), slice(n_in, twice)):
            partner += [jnp.where(low, x[part], y[part]) for x, y in zip(near, far)]
            partner += [jnp.where(low, y[part], x[part]) for x, y in zip(near, far)]
        partner = jnp.concatenate(partner, axis=0)
        first = jnp.concatenate([ref[ch] for ref in blocks], axis=0)
        products = lax.dot_general(
            first, partner, (((1,), (1,)), ((), ())), preferred_element_type=jnp.float32
        )
        for d in range(4):
            at = pl.multiple_of(place[1 + d] * inputs, inputs)
            for q in range(chunks):
                start = (d * chunks + q) * twice
                re = products[start : start + n_in]
                im = products[start + n_in : start + twice]
                rows = pl.ds(at + q * n_in, n_in)
                re_ref[ch, rows, :] = (re[:, :half] + im[:, half:]) * scale
                im_ref[ch, rows, :] = (im[:, :half] - re[:, half:]) * scale


def correlate(place, blocks, swapped, part, parts, before, step=8):
    chunks = len(swapped)
    chans = max(x.shape[0] for x in swapped)
    twice, depth = swapped[0].shape[1:]
    inputs = twice // 2 * chunks
    steps = chans // parts // step
    start = part * steps
    whole = pl.BlockSpec((step, twice, depth), lambda b, place: (b + start, 0, 0))
    own = pl.BlockSpec((step, twice, depth), lambda b, place: (b, 0, 0))
    out = pl.BlockSpec((step, 4 * inputs, 2 * inputs), lambda b, place: (b + start, 0, 0))
    shape = jax.ShapeDtypeStruct((chans, 4 * inputs, 2 * inputs), jnp.float32)
    arrays = [*blocks, *swapped]
    return pl.pallas_call(
        functools.partial(correlate_kernel, chunks, 1.0 / depth),
        grid_spec=pltpu.PrefetchScalarGridSpec(
            num_scalar_prefetch=1,
            grid=(steps,),
            in_specs=[whole if x.shape[0] == chans else own for x in arrays]
            + [pl.BlockSpec(memory_space=pl.ANY)] * len(before),
            out_specs=[out, out],
        ),
        out_shape=[shape, shape],
        input_output_aliases={1 + len(arrays) + j: j for j in range(len(before))},
        compiler_params=pltpu.CompilerParams(vmem_limit_bytes=VMEM),
        cost_estimate=pl.CostEstimate(
            flops=2 * chans // parts * 8 * inputs * 4 * inputs * depth,
            bytes_accessed=36 * 2**20 // parts,
            transcendentals=0,
        ),
        name="correlate",
    )(place, *arrays, *before)


def ring(size, distance):
    return [(i, (i + distance) % size) for i in range(size)]


def shards(voltages, window, table):
    in_dev, frames, length = voltages.shape
    n_freq, n_col = lax.axis_size("freq"), lax.axis_size("col")
    n_in = in_dev // CHUNKS
    back = [(i + 1, i) for i in range(n_freq - 1)]
    row, col = lax.axis_index("row"), lax.axis_index("col")
    up, down = ring(n_col, 1), ring(n_col, -1)

    halos = [lax.ppermute(voltages[q * n_in : (q + 1) * n_in], "freq", back) for q in range(CHUNKS)]
    sent, pieces = [None] * CHUNKS, [None] * CHUNKS

    def front(q, *earlier):
        out = channelize(q, n_in, voltages, halos[q], window, table, earlier)
        sent[q] = lax.all_to_all(out, "freq", split_axis=0, concat_axis=0, tiled=True)
        return out

    def gather(q, *earlier):
        pieces[q] = []
        for block in turn(sent[q], earlier, PARTS if q == CHUNKS - 1 else 1):
            below = lax.ppermute(block, "col", up)
            above = lax.ppermute(block, "col", down)
            if (q + len(pieces[q])) % 2 == 0:
                across = lax.ppermute(below, "col", up)
            else:
                across = lax.ppermute(above, "col", down)
            swapped = lax.ppermute(block, "row", ring(2, 1))
            pieces[q].append((block, below, above, across, swapped))

    front(0)
    gather(0, front(1))
    gather(1, front(2, pieces[0][0][0]))
    gather(2, front(3, pieces[1][0][0], *pieces[0][0][1:3]))
    gather(3, *pieces[1][0][1:3], *pieces[0][0][3:], pieces[2][0][0])
    place = jnp.stack([row, col, (col + 3) % 4, (col + 1) % 4, (col + 2) % 4]).astype(jnp.int32)
    outs = ()
    for part in range(PARTS):
        chosen = [p[part] if len(p) > 1 else p[0] for p in pieces]
        blocks = [chosen[q][d] for d in range(4) for q in range(CHUNKS)]
        swapped = [chosen[q][4] for q in range(CHUNKS)]
        outs = correlate(place, blocks, swapped, part, PARTS, outs)
    return tuple(outs)


def solution(mesh):
    n_freq = mesh.shape["freq"]

    def run(voltages, window):
        table = jnp.asarray(dft_table(voltages.shape[2], n_freq))
        return jax.shard_map(
            shards,
            mesh=mesh,
            in_specs=(P(("row", "col"), "freq", None), P(), P()),
            out_specs=(P("freq", "row", "col"), P("freq", "row", "col")),
            check_vma=False,
        )(voltages, window, table)

    return run
```

```python
import functools
import math

import jax
import jax.numpy as jnp
import ml_dtypes
import numpy as np
from jax import lax
from jax.experimental import pallas as pl
from jax.experimental.pallas import tpu as pltpu
from jax.sharding import PartitionSpec as P

LANES = 128
CHUNKS = 4
PARTS = 2
COPIES = (1, 1, 1, 2)
COLS = 512
SHORT = pl.CostEstimate(flops=10**8, bytes_accessed=2**17, transcendentals=0)
VMEM = 56 * 2**20


def dft_table(length, groups):
    half = length // 2
    base = np.arange(length) * (2.0 * math.pi / length)
    cosine = np.cos(base) / math.sqrt(length)
    sine = -np.sin(base) / math.sqrt(length)
    phase = np.arange(length)[:, None] * np.arange(half)[None, :] % length
    parts = np.stack([cosine[phase], sine[phase]], axis=1)
    parts = parts.reshape(length, 2, groups, half // groups).transpose(0, 2, 1, 3)
    blocks = parts.reshape(length, length // COLS, COLS).transpose(1, 0, 2)
    return blocks.astype(ml_dtypes.bfloat16)


def channelize_kernel(v_ref, h_ref, w_ref, t_ref, *refs):
    u_ref, ext, acc, filt = refs[-4:]
    n_in, frames, length = v_ref.shape
    taps = w_ref.shape[0]
    depth = 2 * frames

    @pl.when(pl.program_id(0) == 0)
    def _():
        def one_tile(t, carry):
            lanes = pl.ds(pl.multiple_of(t * LANES, LANES), LANES)
            for i in range(n_in):
                ext[pl.ds(i * depth, frames), :] = v_ref[i, :, lanes].astype(jnp.float32)
                ext[pl.ds(i * depth + frames, frames), :] = h_ref[i, :, lanes].astype(jnp.float32)
            weights = [jnp.broadcast_to(w_ref[pl.ds(k, 1), lanes], (8, LANES)) for k in range(taps)]
            for i in range(n_in):
                for s in range(0, frames, 8):
                    at = i * depth + s
                    total = weights[0] * ext[pl.ds(at, 8), :]
                    for k in range(1, taps):
                        total = total + weights[k] * ext[pl.ds(at + k, 8), :]
                    acc[pl.ds(i * frames + s, 8), :] = total
            filt[:, lanes] = acc[...].astype(jnp.bfloat16)
            return carry

        lax.fori_loop(0, length // LANES, one_tile, 0)

    out = jnp.dot(filt[...], t_ref[0], preferred_element_type=jnp.float32)
    out = out.astype(jnp.bfloat16)
    for j in range(u_ref.shape[0]):
        for row in range(u_ref.shape[1]):
            u_ref[j, row] = out[:, j * LANES : (j + 1) * LANES].reshape(n_in, frames, LANES)


def channelize(n_in, voltages, v_at, halo, window, table, copies, earlier):
    frames, length = voltages.shape[1:]
    blocks = table.shape[0]
    rows = n_in * frames
    return pl.pallas_call(
        channelize_kernel,
        grid=(blocks,),
        in_specs=[
            pl.BlockSpec((n_in, frames, length), lambda b: (v_at, 0, 0)),
            pl.BlockSpec((n_in, frames, length), lambda b: (0, 0, 0)),
            pl.BlockSpec(window.shape, lambda b: (0, 0)),
            pl.BlockSpec((1, length, COLS), lambda b: (b, 0, 0)),
            *[pl.BlockSpec(memory_space=pl.ANY)] * len(earlier),
        ],
        out_specs=pl.BlockSpec((COLS // LANES, copies, n_in, frames, LANES), lambda b: (b, 0, 0, 0, 0)),
        out_shape=jax.ShapeDtypeStruct((length // LANES, copies, n_in, frames, LANES), jnp.bfloat16),
        scratch_shapes=[
            pltpu.VMEM((2 * rows, LANES), jnp.float32),
            pltpu.VMEM((rows, LANES), jnp.float32),
            pltpu.VMEM((rows, length), jnp.bfloat16),
        ],
        compiler_params=pltpu.CompilerParams(vmem_limit_bytes=VMEM),
        cost_estimate=SHORT,
        name="channelize",
    )(voltages, halo, window, table, *earlier)


def turn_kernel(place, x_ref, *refs):
    g_ref, scr = refs[-2:]
    devices, _, n_in, frames, lanes = x_ref.shape
    chans = lanes // 2
    depth = devices * frames
    for h in range(depth // LANES):
        for i in range(n_in):
            piece = x_ref[h * LANES // frames : (h + 1) * LANES // frames, 0, i, :, :]
            piece = piece.reshape(LANES, lanes).astype(jnp.float32).T
            scr[h, pl.ds(i, chans, stride=2 * n_in), :] = piece[:chans]
            scr[h, pl.ds(n_in + i, chans, stride=2 * n_in), :] = piece[chans:]
        rows = scr[h].reshape(chans, 2 * n_in, LANES)
        g_ref[:, :, h * LANES : (h + 1) * LANES] = rows.astype(jnp.bfloat16)


def turn(received, row_of, place, earlier):
    devices, _, n_in, frames, lanes = received.shape
    chans, depth = lanes // 2, devices * frames
    return pl.pallas_call(
        turn_kernel,
        grid_spec=pltpu.PrefetchScalarGridSpec(
            num_scalar_prefetch=1,
            grid=(1,),
            in_specs=[pl.BlockSpec((devices, 1, n_in, frames, lanes), lambda b, place: (0, row_of(place), 0, 0, 0))]
            + [pl.BlockSpec(memory_space=pl.ANY)] * len(earlier),
            out_specs=pl.BlockSpec((chans, 2 * n_in, depth), lambda b, place: (0, 0, 0)),
            scratch_shapes=[pltpu.VMEM((depth // LANES, chans * 2 * n_in, LANES), jnp.float32)],
        ),
        out_shape=jax.ShapeDtypeStruct((chans, 2 * n_in, depth), jnp.bfloat16),
        compiler_params=pltpu.CompilerParams(vmem_limit_bytes=VMEM),
        cost_estimate=SHORT,
        name="turn",
    )(place, received, *earlier)


def correlate_kernel(chunks, scale, place, *refs):
    blocks, far_refs = refs[: 4 * chunks], refs[4 * chunks : 5 * chunks]
    near_refs = blocks[:chunks]
    re_ref, im_ref = refs[-2:]
    chans, twice, depth = blocks[0].shape
    n_in = twice // 2
    inputs = n_in * chunks
    half = 2 * inputs

    def channels(lower, upper):
        for ch in range(chans):
            partner = [ref[ch, part] for part in (slice(0, n_in), slice(n_in, twice)) for ref in (*lower, *upper)]
            partner = jnp.concatenate(partner, axis=0)
            first = jnp.concatenate([ref[ch] for ref in blocks], axis=0)
            products = lax.dot_general(
                first, partner, (((1,), (1,)), ((), ())), preferred_element_type=jnp.float32
            )
            for d in range(4):
                at = pl.multiple_of(place[1 + d] * inputs, inputs)
                for q in range(chunks):
                    start = (d * chunks + q) * twice
                    re = products[start : start + n_in]
                    im = products[start + n_in : start + twice]
                    rows = pl.ds(at + q * n_in, n_in)
                    re_ref[ch, rows, :] = (re[:, :half] + im[:, half:]) * scale
                    im_ref[ch, rows, :] = (im[:, :half] - re[:, half:]) * scale

    pl.when(place[0] == 0)(lambda: channels(near_refs, far_refs))
    pl.when(place[0] == 1)(lambda: channels(far_refs, near_refs))


def correlate(place, gathered, far, part, parts, before, step=8):
    chunks = len(far)
    chans, twice, depth = far[0].shape
    inputs = twice // 2 * chunks
    steps = chans // parts // step
    start = part * steps
    whole = pl.BlockSpec((step, twice, depth), lambda b, place: (b + start, 0, 0))
    own = pl.BlockSpec((step, twice, depth), lambda b, place: (b, 0, 0))
    out = pl.BlockSpec((step, 4 * inputs, 2 * inputs), lambda b, place: (b + start, 0, 0))
    shape = jax.ShapeDtypeStruct((chans, 4 * inputs, 2 * inputs), jnp.float32)
    arrays = [x for group in gathered for x in group] + far
    return pl.pallas_call(
        functools.partial(correlate_kernel, chunks, 1.0 / depth),
        grid_spec=pltpu.PrefetchScalarGridSpec(
            num_scalar_prefetch=1,
            grid=(steps,),
            in_specs=[whole if x.shape[0] == chans else own for x in arrays]
            + [pl.BlockSpec(memory_space=pl.ANY)] * len(before),
            out_specs=[out, out],
        ),
        out_shape=[shape, shape],
        input_output_aliases={1 + len(arrays) + j: j for j in range(len(before))},
        compiler_params=pltpu.CompilerParams(vmem_limit_bytes=VMEM),
        cost_estimate=SHORT,
        name="correlate",
    )(place, *arrays, *before)


def ring(size, distance):
    return [(i, (i + distance) % size) for i in range(size)]


def after(x, *earlier):
    return lax.optimization_barrier((x, *earlier))[0]


def shards(voltages, window, table):
    in_dev, frames, length = voltages.shape
    n_freq, n_col = lax.axis_size("freq"), lax.axis_size("col")
    n_in = in_dev // CHUNKS
    back = [(i + 1, i) for i in range(n_freq - 1)]
    row, col = lax.axis_index("row"), lax.axis_index("col")
    place = jnp.stack([row, col, (col + 3) % 4, (col + 1) % 4, (col + 2) % 4]).astype(jnp.int32)
    up, down = ring(n_col, 1), ring(n_col, -1)

    pieces = [voltages[:n_in]]
    rest = after(voltages, pieces[0])
    pieces += [rest[q * n_in : (q + 1) * n_in] for q in range(1, CHUNKS)]
    halos = []
    for q, waits in enumerate(((), (0,), (0,), (1,))):
        halos.append(lax.ppermute(after(pieces[q], *[halos[j] for j in waits]), "freq", back))
    sent, near, below, above, across, far = [[] for _ in range(6)]

    def front(q, *earlier):
        return channelize(n_in, voltages, q, halos[q], window, table, COPIES[q], earlier)

    def exchange(q, out):
        flat = out.reshape(n_freq * COPIES[q], *out.shape[2:])
        axes = "freq" if COPIES[q] == 1 else ("freq", "row")
        sent.append(lax.all_to_all(flat, axes, 0, 0, tiled=True).reshape(out.shape))

    def gather(q, *earlier):
        both = COPIES[q] == 2
        block = turn(sent[q], lambda place: place[0] if both else 0, place, earlier)
        near.append(block)
        free = after(block, *below[-1:], *above[-1:], *(across[q - 2] if q >= 2 else ()))
        below.append(lax.ppermute(free, "col", up))
        above.append(lax.ppermute(free, "col", down))
        part = block.shape[0] // PARTS
        if q < CHUNKS - 2:
            across.append([lax.ppermute(below[q][:part], "col", up), lax.ppermute(above[q][part:], "col", down)])

    def swap(q, *earlier):
        far.append(lax.ppermute(after(near[q], *earlier), "row", ring(2, 1)))

    def onward(q, j, *earlier):
        part = near[q].shape[0] // PARTS
        at = j * part
        source = below[q][at : at + part // 2], above[q][at + part // 2 : at + part]
        source = [after(x, *earlier) for x in source]
        return lax.ppermute(source[0], "col", up), lax.ppermute(source[1], "col", down)

    def cross(q, *earlier):
        far.append(turn(sent[q], lambda place: 1 - place[0], place, earlier))

    exchange(0, front(0))
    out = front(1)
    exchange(1, out)
    gather(0, out)
    swap(0, halos[-1])
    out = front(2, near[0])
    exchange(2, out)
    gather(1, out)
    out = front(3, near[1])
    exchange(3, out)
    gather(2, out, far[0])
    first = onward(2, 0)
    swap(1, sent[3])
    swap(2, sent[3])
    cross(3, near[2])
    gather(3, near[2], far[3])
    second = onward(3, 0, *first, far[1])
    third = onward(2, 1, *second, far[1])
    fourth = onward(3, 1, *second)
    across += [[jnp.concatenate(x, axis=0) for x in (first, third)], [jnp.concatenate(x, axis=0) for x in (second, fourth)]]
    outs = ()
    for part in range(PARTS):
        gathered = [near, below, above, [x[part] if isinstance(x, list) else x for x in across]]
        outs = correlate(place, gathered, far, part, PARTS, outs)
    return tuple(outs)


def solution(mesh):
    n_freq = mesh.shape["freq"]

    def run(voltages, window):
        table = jnp.asarray(dft_table(voltages.shape[2], n_freq))
        return jax.shard_map(
            shards,
            mesh=mesh,
            in_specs=(P(("row", "col"), "freq", None), P(), P()),
            out_specs=(P("freq", "row", "col"), P("freq", "row", "col")),
            check_vma=False,
        )(voltages, window, table)

    return run
```
